256 devices in a mesh: inp: 8 (over z), wgt: 8 (over x_lo, y), out: 4 (over x_hi, core).
Axes of the slice: x: 4 (x_hi: 2, x_lo: 2; x = x_hi * 2 + x_lo), y: 4, z: 8, core: 2. Of those that a mesh axis runs over, the one named last changes fastest.
Arguments:
- tokens: bfloat16 [1024, 6144], P('out', ('wgt', 'inp')), may hold values from -6 to 6
- w_up: bfloat16 [6144, 24576], P(('wgt', 'out'), 'inp'), may hold values from -0.078125 to 0.078125
- w_down: bfloat16 [24576, 6144], P(('inp', 'out'), 'wgt'), may hold values from -0.0390625 to 0.0390625
- grad_out: bfloat16 [1024, 6144], P('out', ('wgt', 'inp')), may hold values from -6 to 6
Outputs:
- output: bfloat16 [1024, 6144], P('out', ('wgt', 'inp'))
- grad_tokens: bfloat16 [1024, 6144], P('out', ('wgt', 'inp'))
- grad_up: bfloat16 [6144, 24576], P(('wgt', 'out'), 'inp')
- grad_down: bfloat16 [24576, 6144], P(('inp', 'out'), 'wgt')
The draws below stay inside these ranges and needn't reach their ends.
All inputs are finite; a program needn't handle non-finite values.
Results may differ from the reference program's by a relative error of at most 0.029.
Values may be sent and summed in bfloat16 or wider, within the bound.
No kernel may reach another device: no remote copies, remote signals or barrier semaphores. Data moves between devices by JAX's collectives and lax.ppermute only.
A program may use at most 64 MiB of HBM per device.

```python
import jax
import jax.numpy as jnp
from jax import lax

D = 6144
FF = 24576
TOKENS = 1024
N_INP = 8
N_WGT = 8
N_OUT = 4


def level_of(key, extent, split, low, high):
    factor_of = 1.0
    for position, parts in split:
        draws = jax.random.uniform(jax.random.fold_in(jax.random.fold_in(key, 6), position), (parts,), jnp.float32, low / len(split), high / len(split))
        factor_of = factor_of * jnp.repeat(jnp.exp(draws), extent[position] // parts).reshape((-1,) + (1,) * (len(extent) - 1 - position))
    return factor_of


def scatter_about(stream_key, dims, deviation, most, shards=(), kind=jnp.bfloat16):
    array = jax.random.normal(stream_key, dims, jnp.float32) * deviation
    if len(shards) > 0:
        array = level_of(stream_key, dims, shards, -0.22, 0.18) * array
    return jnp.clip(array, min=-most, max=most).astype(kind)


def setup_inputs(seed: int = 0) -> dict:
    seeds = jax.random.split(jax.random.key(seed), 5)
    tokens = scatter_about(seeds[0], (TOKENS, D), 1.0, 6.0, ((0, 4), (1, 64)))
    w_up = scatter_about(seeds[1], (D, FF), D ** -0.5, 0.078125, ((0, 32), (1, 8)))
    w_down = scatter_about(seeds[2], (FF, D), FF ** -0.5, 0.0390625, ((0, 32), (1, 8)))
    grad_out = scatter_about(seeds[3], (TOKENS, D), 1.0, 6.0, ((0, 4), (1, 64)))
    return {"tokens": tokens, "w_up": w_up, "w_down": w_down, "grad_out": grad_out}


tanh_scale = 0.7978845608028654
cubic_weight = 0.044715


def gelu_value(hidden):
    tangent = jnp.tanh(tanh_scale * (hidden + cubic_weight * hidden * hidden * hidden))
    return 0.5 * hidden * (1.0 + tangent)


def gelu_slope(hidden):
    tangent = jnp.tanh(tanh_scale * (hidden + cubic_weight * hidden * hidden * hidden))
    return 0.5 * (1.0 + tangent) + 0.5 * hidden * (1.0 - tangent * tangent) * tanh_scale * (1.0 + 3.0 * cubic_weight * hidden * hidden)


def blocked(former, latter, blocks):
    block_width = former.shape[1] // blocks

    def accumulate(block_index, running):
        offset = (block_index * block_width).astype(jnp.int32)
        former_block = lax.dynamic_slice_in_dim(former, offset, block_width, 1)
        latter_block = lax.dynamic_slice_in_dim(latter, offset, block_width, 0)
        partial_value = jnp.dot(former_block, latter_block, preferred_element_type=jnp.float32).astype(jnp.bfloat16)
        partial_value = lax.optimization_barrier(partial_value)
        return running + partial_value.astype(jnp.float32)

    start_value = jnp.zeros((former.shape[0], latter.shape[1]), jnp.float32)
    return lax.fori_loop(0, blocks, accumulate, start_value)


def reference(tokens, w_up, w_down, grad_out):
    hidden = blocked(tokens, w_up, N_WGT)
    activation = gelu_value(hidden).astype(jnp.bfloat16)
    output = blocked(activation, w_down, N_INP).astype(jnp.bfloat16)
    grad_act = blocked(grad_out, w_down.T, N_WGT)
    grad_hidden = (grad_act * gelu_slope(hidden)).astype(jnp.bfloat16)
    grad_tokens = blocked(grad_hidden, w_up.T, N_INP).astype(jnp.bfloat16)
    grad_down = blocked(activation.T, grad_out, N_OUT).astype(jnp.bfloat16)
    grad_up = blocked(tokens.T, grad_hidden, N_OUT).astype(jnp.bfloat16)
    return output, grad_tokens, grad_up, grad_down
```

```python
import jax
import jax.numpy as jnp
import numpy as np
from jax import lax
from jax.sharding import Mesh, PartitionSpec as P

tanh_scale = 0.7978845608028654
cubic_weight = 0.044715
pair = [(0, 1), (1, 0)]


def gelu_both(hidden):
    tangent = jnp.tanh(tanh_scale * (hidden + cubic_weight * hidden * hidden * hidden))
    value = 0.5 * hidden * (1.0 + tangent)
    slope = 0.5 * (1.0 + tangent) + 0.5 * hidden * (1.0 - tangent * tangent) * tanh_scale * (
        1.0 + 3.0 * cubic_weight * hidden * hidden
    )
    return value, slope


def contract(former, latter, former_dim, latter_dim):
    return lax.dot_general(
        former,
        latter,
        (((former_dim,), (latter_dim,)), ((), ())),
        preferred_element_type=jnp.float32,
    ).astype(jnp.bfloat16)


def swap(value, axis):
    return lax.ppermute(value, axis, pair)


def exchange(value, axis):
    return lax.all_to_all(value, axis, 0, 0, tiled=True)


def spread(value, axis, count):
    copies = jnp.broadcast_to(value[None], (count,) + value.shape)
    return exchange(copies, axis)


def share(value, axis, count):
    blocks = exchange(value.reshape((count, value.shape[0] // count) + value.shape[1:]), axis)
    return jnp.sum(blocks.astype(jnp.float32), axis=0)


def gathered(own):
    beside = swap(own, "core")
    across = swap(own, "xhi")
    beyond = swap(across, "core")
    return jnp.concatenate([beside, beyond, own, across], axis=0)


def scattered(former, latter, latter_dim):
    half = former.shape[0] // 2
    quarter = half // 2
    outgoing = contract(former[:half], latter, 1, latter_dim)
    kept = contract(former[half:], latter, 1, latter_dim)
    arrived = swap(outgoing, "core")
    total = kept.astype(jnp.float32) + arrived.astype(jnp.float32)
    crossing = swap(total[quarter:].astype(jnp.bfloat16), "xhi")
    return (total[:quarter] + crossing.astype(jnp.float32)).astype(jnp.bfloat16)


def orders(here):
    forth = [here ^ 1, here ^ 3, here, here ^ 2]
    back = [2 * (1 - ((here ^ j) & 1)) + ((here ^ j) >> 1) for j in range(4)]
    return forth, back


def reordered(array, blocks):
    size = array.shape[0] // 4
    return jnp.concatenate(
        [lax.dynamic_slice_in_dim(array, block * size, size, 0) for block in blocks], axis=0
    )


def per_device(tokens, w_up, w_down, grad_out):
    xhi, core = lax.axis_index("xhi"), lax.axis_index("core")
    blocks, places = orders(2 * xhi + core)
    up = gathered(w_up)
    down = gathered(w_down)
    both = jnp.concatenate([tokens.T, grad_out.T], axis=0)
    features = spread(both, "inp", 8).reshape(8, 2, 96, 256)
    x = reordered(features[:, 0].reshape(768, 256), blocks)
    g = features[:, 1].reshape(768, 256)

    hidden = share(contract(up, x, 0, 0), ("xlo", "y"), 8)
    value, slope = gelu_both(hidden)
    act = spread(value.astype(jnp.bfloat16), ("xlo", "y"), 8).reshape(3072, 256)

    grad_act_partial = contract(down, g, 1, 0)
    grad_act_rows = reordered(grad_act_partial, places)
    grad_act = share(grad_act_rows, ("xlo", "y"), 8)
    gh = spread((grad_act * slope).astype(jnp.bfloat16), ("xlo", "y"), 8).reshape(3072, 256)

    act_r = reordered(act, blocks)
    out = share(contract(down, act_r, 0, 0), "inp", 8).astype(jnp.bfloat16)
    grad_tok_partial = reordered(contract(up, gh, 1, 0), places)
    grad_tok = share(grad_tok_partial, "inp", 8).astype(jnp.bfloat16)
    grad_down = scattered(act_r, g, 1)
    grad_up = scattered(x, gh, 1)
    return (out.T, grad_tok.T, grad_up, grad_down)


def solution(mesh):
    fine = Mesh(
        np.asarray(mesh.devices).reshape(8, 2, 4, 2, 2), ("inp", "xlo", "y", "xhi", "core")
    )
    wgt, out = ("xlo", "y"), ("xhi", "core")
    tok = P(out, wgt + ("inp",))
    up = P(wgt + out, "inp")
    down = P(("inp",) + out, wgt)
    return jax.shard_map(
        per_device,
        mesh=fine,
        in_specs=(tok, up, down, tok),
        out_specs=(tok, tok, up, down),
        check_vma=False,
    )
```

```python
import jax
import jax.numpy as jnp
import numpy as np
from jax import lax
from jax.sharding import Mesh, PartitionSpec as P

tanh_scale = 0.7978845608028654
cubic_weight = 0.044715
pair = [(0, 1), (1, 0)]


def gelu_both(hidden):
    tangent = jnp.tanh(tanh_scale * (hidden + cubic_weight * hidden * hidden * hidden))
    value = 0.5 * hidden * (1.0 + tangent)
    slope = 0.5 * (1.0 + tangent) + 0.5 * hidden * (1.0 - tangent * tangent) * tanh_scale * (
        1.0 + 3.0 * cubic_weight * hidden * hidden
    )
    return value, slope


def contract(former, latter, former_dim, latter_dim):
    return lax.dot_general(
        former,
        latter,
        (((former_dim,), (latter_dim,)), ((), ())),
        preferred_element_type=jnp.float32,
    ).astype(jnp.bfloat16)


def swap(value, axis):
    return lax.ppermute(value, axis, pair)


def exchange(value, axis):
    return lax.all_to_all(value, axis, 0, 0, tiled=True)


def spread(value, axis, count):
    copies = jnp.broadcast_to(value[None], (count,) + value.shape)
    return exchange(copies, axis)


def share(value, axis, count):
    blocks = exchange(value.reshape((count, value.shape[0] // count) + value.shape[1:]), axis)
    return jnp.sum(blocks.astype(jnp.float32), axis=0)


def gathered(own):
    beside = swap(own, "core")
    across = swap(own, "xhi")
    beyond = swap(across, "core")
    return jnp.concatenate([beside, beyond, own, across], axis=0)


def scattered(former, latter, latter_dim):
    half = former.shape[0] // 2
    quarter = half // 2
    outgoing = contract(former[:half], latter, 1, latter_dim)
    kept = contract(former[half:], latter, 1, latter_dim)
    arrived = swap(outgoing, "core")
    total = kept.astype(jnp.float32) + arrived.astype(jnp.float32)
    crossing = swap(total[quarter:].astype(jnp.bfloat16), "xhi")
    return (total[:quarter] + crossing.astype(jnp.float32)).astype(jnp.bfloat16)


def orders(here):
    forth = [here ^ 1, here ^ 3, here, here ^ 2]
    back = [2 * (1 - ((here ^ j) & 1)) + ((here ^ j) >> 1) for j in range(4)]
    return forth, back


def reordered(array, blocks):
    size = array.shape[0] // 4
    return jnp.concatenate(
        [lax.dynamic_slice_in_dim(array, block * size, size, 0) for block in blocks], axis=0
    )


def natural(own, other, place):
    return jnp.where(place == 0, jnp.stack([own, other]), jnp.stack([other, own]))


def pick(array, place):
    return lax.dynamic_index_in_dim(array, place, 0, keepdims=False)


def per_device(tokens, w_up, w_down, grad_out):
    xhi, core = lax.axis_index("xhi"), lax.axis_index("core")
    blocks, places = orders(2 * xhi + core)
    wgt = ("xlo", "y")
    both = jnp.concatenate([tokens.T, grad_out.T], axis=0)
    features = spread(both, "inp", 8).reshape(8, 2, 96, 256)
    up = gathered(w_up)
    down = natural(w_down, swap(w_down, "core"), core).reshape(1536, 768)
    x = reordered(features[:, 0].reshape(768, 256), blocks)
    g_own = features[:, 1].reshape(768, 256)
    g = natural(g_own, swap(g_own, "xhi"), xhi)

    hidden_partial = contract(up, x, 0, 0).reshape(2, 8, 192, 256).transpose(1, 0, 2, 3)
    hidden = share(hidden_partial.reshape(3072, 256), wgt, 8).reshape(2, 192, 256)
    value, slope = gelu_both(hidden)
    value = value.astype(jnp.bfloat16)

    act_partial = jnp.stack(
        [contract(down, g[half], 1, 0).reshape(8, 192, 256) for half in range(2)]
    )
    payload = jnp.concatenate(
        [act_partial, jnp.broadcast_to(value[:, None], (2, 8, 192, 256))], axis=2
    )
    arrived = exchange(payload.reshape(16, 384, 256), ("xhi",) + wgt).reshape(2, 8, 2, 192, 256)
    grad_act = jnp.sum(arrived[:, :, 0].astype(jnp.float32), axis=1)
    act = arrived[:, :, 1].reshape(2, 1536, 256)

    gh = spread((grad_act * slope).astype(jnp.bfloat16), wgt, 8)
    gh = gh.transpose(1, 0, 2, 3).reshape(3072, 256)

    out_own = contract(down, pick(act, xhi), 0, 0)
    out_other = swap(contract(down, pick(act, 1 - xhi), 0, 0), "xhi")
    out = (out_own.astype(jnp.float32) + out_other.astype(jnp.float32)).astype(jnp.bfloat16)

    act_wide = jnp.concatenate([act[0], act[1]], axis=1)
    g_wide = jnp.concatenate([g[0], g[1]], axis=1)
    act_far = lax.dynamic_slice_in_dim(act_wide, (1 - core) * 768, 768, 0)
    act_near = lax.dynamic_slice_in_dim(act_wide, core * 768, 768, 0)
    down_far = swap(contract(act_far, g_wide, 1, 1), "core")
    down_near = contract(act_near, g_wide, 1, 1)
    grad_down = (down_near.astype(jnp.float32) + down_far.astype(jnp.float32)).astype(jnp.bfloat16)

    grad_tok = reordered(contract(up, gh, 1, 0), places)
    last = jnp.concatenate([out.reshape(8, 96, 256), grad_tok.reshape(8, 96, 256)], axis=1)
    last = share(last.reshape(1536, 256), "inp", 8).astype(jnp.bfloat16)
    grad_up = scattered(x, gh, 1)
    return (last[:96].T, last[96:].T, grad_up, grad_down)


def solution(mesh):
    fine = Mesh(
        np.asarray(mesh.devices).reshape(8, 2, 4, 2, 2), ("inp", "xlo", "y", "xhi", "core")
    )
    wgt, out = ("xlo", "y"), ("xhi", "core")
    tok = P(out, wgt + ("inp",))
    up = P(wgt + out, "inp")
    down = P(("inp",) + out, wgt)
    return jax.shard_map(
        per_device,
        mesh=fine,
        in_specs=(tok, up, down, tok),
        out_specs=(tok, tok, up, down),
        check_vma=False,
    )
```

```python
import jax
import jax.numpy as jnp
import numpy as np
from jax import lax
from jax.experimental import pallas as pl
from jax.experimental.pallas import tpu as pltpu
from jax.sharding import Mesh, PartitionSpec as P

tanh_scale = 0.7978845608028654
cubic_weight = 0.044715
pair = [(0, 1), (1, 0)]
wgt = ("xlo", "y")
bf16, f32 = jnp.bfloat16, jnp.float32


def gelu_both(hidden):
    tangent = jnp.tanh(tanh_scale * (hidden + cubic_weight * hidden * hidden * hidden))
    value = 0.5 * hidden * (1.0 + tangent)
    slope = 0.5 * (1.0 + tangent) + 0.5 * hidden * (1.0 - tangent * tangent) * tanh_scale * (
        1.0 + 3.0 * cubic_weight * hidden * hidden
    )
    return value, slope


def dot(former, latter, former_dim, latter_dim):
    return lax.dot_general(
        former,
        latter,
        (((former_dim,), (latter_dim,)), ((), ())),
        preferred_element_type=f32,
    )


def contract(former, latter, former_dim, latter_dim):
    return dot(former, latter, former_dim, latter_dim).astype(bf16)


def swap(value, axis):
    return lax.ppermute(value, axis, pair)


def exchange(value, axis):
    return lax.all_to_all(value, axis, 0, 0, tiled=True)


def natural(own, other, place):
    return jnp.where(place == 0, jnp.stack([own, other]), jnp.stack([other, own]))


def local(kernel, outs, flops, moved, *operands):
    whole = pl.BlockSpec(memory_space=pltpu.VMEM)
    return pl.pallas_call(
        kernel,
        out_shape=[jax.ShapeDtypeStruct(shape, kind) for shape, kind in outs],
        in_specs=[pl.BlockSpec(memory_space=pltpu.SMEM)] + [whole] * (len(operands) - 1),
        out_specs=[whole] * len(outs),
        compiler_params=pltpu.CompilerParams(vmem_limit_bytes=40 * 1024 * 1024),
        cost_estimate=pl.CostEstimate(flops=flops, bytes_accessed=moved, transcendentals=0),
    )(*operands)


def feature_rows(features, block):
    return features[pl.ds(2 * block, 2), 0:96, :].reshape(192, 256)


def hidden_kernel(where, features, w0, w1, w2, w3, out):
    turned = [feature_rows(features, where[b]).T for b in range(4)]
    for chunk in range(8):
        columns = slice(384 * chunk, 384 * chunk + 384)
        total = dot(turned[0], w0[:, columns], 1, 0)
        for b, weights in ((1, w1), (2, w2), (3, w3)):
            total += dot(turned[b], weights[:, columns], 1, 0)
        rows = total.T.astype(bf16)
        half, target = chunk // 4, 2 * (chunk % 4)
        span = slice(192 * half, 192 * half + 192)
        out[target, span, :] = rows[:192]
        out[target + 1, span, :] = rows[192:]


def gelu_kernel(where, arrived, first, second, payload, slopes):
    for half, partial_sums in ((0, first), (1, second)):
        span = slice(192 * half, 192 * half + 192)
        hidden = arrived[0, span, :].astype(f32)
        for source in range(1, 8):
            hidden += arrived[source, span, :].astype(f32)
        value, slope = gelu_both(hidden)
        value = value.astype(bf16)
        slopes[span, :] = slope
        for target in range(8):
            payload[8 * half + target, 0:192, :] = partial_sums[192 * target : 192 * target + 192, :]
            payload[8 * half + target, 192:384, :] = value


def slope_kernel(where, arrived, slopes, copies):
    for half in range(2):
        span = slice(192 * half, 192 * half + 192)
        total = arrived[8 * half, 0:192, :].astype(f32)
        for source in range(1, 8):
            total += arrived[8 * half + source, 0:192, :].astype(f32)
        gradient = (total * slopes[span, :]).astype(bf16)
        for target in range(8):
            copies[target, span, :] = gradient


def hidden_rows(gathered, chunk):
    half, source = chunk // 4, 2 * (chunk % 4)
    span = slice(192 * half, 192 * half + 192)
    return jnp.concatenate([gathered[source, span, :], gathered[source + 1, span, :]], axis=0)


def products_kernel(where, arrived, down, cotangents, out, down_grad):
    tokens_of, rows_of = where[0], where[1]
    total = dot(down[0:192, :], arrived[8 * tokens_of, 192:384, :], 0, 0)
    for block in range(1, 8):
        hidden = arrived[8 * tokens_of + block, 192:384, :]
        total += dot(down[192 * block : 192 * block + 192, :], hidden, 0, 0)
    out[...] = total.astype(bf16)
    for block in range(4):
        total = dot(arrived[4 * rows_of + block, 192:384, :], cotangents[0], 1, 1)
        total += dot(arrived[8 + 4 * rows_of + block, 192:384, :], cotangents[1], 1, 1)
        down_grad[192 * block : 192 * block + 192, :] = total.astype(bf16)


def rows_kernel(where, features, gathered, sent, kept):
    rows_of = jnp.concatenate(
        [feature_rows(features, where[0]), feature_rows(features, where[1])], axis=0
    )
    for chunk in range(8):
        rows = hidden_rows(gathered, chunk)
        columns = slice(384 * chunk, 384 * chunk + 384)
        total = dot(rows_of, rows, 1, 1).astype(bf16)
        sent[:, columns] = total[:192]
        kept[:, columns] = total[192:]


def tokens_kernel(where, gathered, w0, w1, w2, w3, own, other, payload):
    total = own[...].astype(f32) + other[...].astype(f32)
    payload[:, 0:96, :] = total.astype(bf16).reshape(8, 96, 256)
    rows = [hidden_rows(gathered, chunk) for chunk in range(8)]
    for b, weights in enumerate((w0, w1, w2, w3)):
        total = dot(weights[:, 0:384], rows[0], 1, 0)
        for chunk in range(1, 8):
            total += dot(weights[:, 384 * chunk : 384 * chunk + 384], rows[chunk], 1, 0)
        payload[pl.ds(2 * where[b], 2), 96:192, :] = total.astype(bf16).reshape(2, 96, 256)


def per_device(tokens, w_up, w_down, grad_out):
    xhi, core = lax.axis_index("xhi"), lax.axis_index("core")
    here = (2 * xhi + core).astype(jnp.int32)
    places = jnp.stack([here, here ^ 1, here ^ 2, here ^ 3])
    far_places = jnp.stack([here ^ 3, here ^ 2])
    near_places = jnp.stack([here ^ 1, here])

    up_across = swap(w_up, "xhi")
    up_beside = swap(w_up, "core")
    up_beyond = swap(up_across, "core")
    up = (w_up, up_beside, up_across, up_beyond)
    both = jnp.concatenate([tokens.T, grad_out.T], axis=0)
    features = exchange(jnp.broadcast_to(both[None], (8, 192, 256)), "inp")
    down = natural(w_down, swap(w_down, "core"), core).reshape(1536, 768)
    g_own = features[:, 96:].reshape(768, 256)
    g_other = swap(g_own, "xhi")

    (hidden_partial,) = local(
        hidden_kernel, [((8, 384, 256), bf16)], 1 << 30, 7 << 20, places, features, *up
    )
    hidden_partial, g_own, g_other = lax.optimization_barrier((hidden_partial, g_own, g_other))
    hidden = exchange(hidden_partial, wgt)
    g = natural(g_own, g_other, xhi)
    payload, slopes = local(
        gelu_kernel,
        [((16, 384, 256), bf16), ((384, 256), f32)],
        1 << 24,
        6 << 20,
        places,
        hidden,
        contract(down, g[0], 1, 0),
        contract(down, g[1], 1, 0),
    )
    arrived = exchange(payload, ("xhi",) + wgt)
    (copies,) = local(
        slope_kernel, [((8, 384, 256), bf16)], 1 << 22, 3 << 20, places, arrived, slopes
    )
    copies, arrived = lax.optimization_barrier((copies, arrived))
    gh = exchange(copies, wgt)

    core_place = jnp.stack([xhi, core]).astype(jnp.int32)
    shapes = [((768, 256), bf16), ((768, 768), bf16)]
    turned = (1 - core_place).astype(jnp.int32)
    out_sent, down_sent = local(products_kernel, shapes, 1 << 20, 1 << 16, turned, arrived, down, g)
    out_other, down_far = swap(out_sent, "xhi"), swap(down_sent, "core")
    out_own, down_near = local(
        products_kernel, shapes, 1 << 20, 1 << 16, core_place, arrived, down, g
    )
    grad_down = (down_near.astype(f32) + down_far.astype(f32)).astype(bf16)
    gh, out_own, grad_down = lax.optimization_barrier((gh, out_own, grad_down))

    row_outs = [((192, 3072), bf16)] * 2
    sent, kept = local(rows_kernel, row_outs, 1 << 29, 4 << 20, far_places, features, gh)
    sent, kept, out_other = lax.optimization_barrier((sent, kept, out_other))
    crossing = (kept.astype(f32) + swap(sent, "core").astype(f32)).astype(bf16)
    (last,) = local(
        tokens_kernel, [((8, 192, 256), bf16)], 1 << 30, 7 << 20, places, gh, *up, out_own, out_other
    )
    last, crossing, gh = lax.optimization_barrier((last, crossing, gh))
    crossed = swap(crossing, "xhi")
    last = exchange(last, "inp")
    sums = jnp.sum(last.astype(f32), axis=0).astype(bf16)
    sent, kept = local(rows_kernel, row_outs, 1 << 29, 4 << 20, near_places, features, gh)
    near = kept.astype(f32) + swap(sent, "core").astype(f32)
    grad_up = (near + crossed.astype(f32)).astype(bf16)
    return (sums[:96].T, sums[96:].T, grad_up, grad_down)


def solution(mesh):
    fine = Mesh(
        np.asarray(mesh.devices).reshape(8, 2, 4, 2, 2), ("inp", "xlo", "y", "xhi", "core")
    )
    out = ("xhi", "core")
    tok = P(out, wgt + ("inp",))
    up = P(wgt + out, "inp")
    down = P(("inp",) + out, wgt)
    return jax.shard_map(
        per_device,
        mesh=fine,
        in_specs=(tok, up, down, tok),
        out_specs=(tok, tok, up, down),
        check_vma=False,
    )
```

```python
import jax
import jax.numpy as jnp
import numpy as np
from jax import lax
from jax.experimental import pallas as pl
from jax.experimental.pallas import tpu as pltpu
from jax.sharding import Mesh, PartitionSpec as P

tanh_scale = 0.7978845608028654
cubic_weight = 0.044715
pair = [(0, 1), (1, 0)]
wgt = ("xlo", "y")
bf16, f32 = jnp.bfloat16, jnp.float32


def gelu_both(hidden):
    tangent = jnp.tanh(tanh_scale * (hidden + cubic_weight * hidden * hidden * hidden))
    value = 0.5 * hidden * (1.0 + tangent)
    slope = 0.5 * (1.0 + tangent) + 0.5 * hidden * (1.0 - tangent * tangent) * tanh_scale * (
        1.0 + 3.0 * cubic_weight * hidden * hidden
    )
    return value, slope


def dot(former, latter, former_dim, latter_dim):
    return lax.dot_general(
        former,
        latter,
        (((former_dim,), (latter_dim,)), ((), ())),
        preferred_element_type=f32,
    )


def swap(value, axis):
    return lax.ppermute(value, axis, pair)


def exchange(value, axis):
    return lax.all_to_all(value, axis, 0, 0, tiled=True)


def natural(own, other, place):
    return jnp.where(place == 0, jnp.stack([own, other]), jnp.stack([other, own]))


def local(kernel, outs, *operands, kinds=None, flops=1 << 20):
    whole = pl.BlockSpec(memory_space=pltpu.VMEM)
    kinds = kinds or [bf16] * len(outs)
    return pl.pallas_call(
        kernel,
        out_shape=[jax.ShapeDtypeStruct(shape, kind) for shape, kind in zip(outs, kinds)],
        in_specs=[pl.BlockSpec(memory_space=pltpu.SMEM)] + [whole] * (len(operands) - 1),
        out_specs=[whole] * len(outs),
        compiler_params=pltpu.CompilerParams(vmem_limit_bytes=16 * 1024 * 1024),
        cost_estimate=pl.CostEstimate(flops=flops, bytes_accessed=1 << 16, transcendentals=0),
    )(*operands)


def feature_rows(features, block):
    return features[pl.ds(2 * block, 2), 0:96, :].reshape(192, 256)


def hidden_kernel(where, features, w0, w1, w2, w3, out):
    turned = [feature_rows(features, where[b]).T for b in range(4)]
    for chunk in range(8):
        columns = slice(384 * chunk, 384 * chunk + 384)
        total = dot(turned[0], w0[:, columns], 1, 0)
        for b, weights in ((1, w1), (2, w2), (3, w3)):
            total += dot(turned[b], weights[:, columns], 1, 0)
        rows = total.astype(bf16).T
        half, target = chunk // 4, 2 * (chunk % 4)
        span = slice(192 * half, 192 * half + 192)
        out[target, span, :] = rows[:192]
        out[target + 1, span, :] = rows[192:]


def partial_kernel(where, down, own, other, partial_sums):
    for side, cotangents in ((where[0], own), (1 - where[0], other)):
        for block in range(8):
            rows = down[192 * block : 192 * block + 192, :]
            partial_sums[side, block] = dot(rows, cotangents[...], 1, 0).astype(bf16)


def gelu_kernel(where, arrived, values, slopes):
    for half in range(2):
        span = slice(192 * half, 192 * half + 192)
        hidden = arrived[0, span, :].astype(f32)
        for source in range(1, 8):
            hidden += arrived[source, span, :].astype(f32)
        value, slope = gelu_both(hidden)
        values[half] = value.astype(bf16)
        slopes[span, :] = slope


def output_kernel(where, gathered, down, own, sent):
    for result, first in ((sent, 576), (own, 384)):
        total = dot(down[0:192, :], gathered[0, first : first + 192, :], 0, 0)
        for block in range(1, 8):
            hidden = gathered[block, first : first + 192, :]
            total += dot(down[192 * block : 192 * block + 192, :], hidden, 0, 0)
        result[...] = total.astype(bf16)


def down_kernel(where, gathered, own, other, sent, kept):
    for result, rows_of in ((sent, 1 - where[1]), (kept, where[1])):
        for block in range(4):
            place = 4 * rows_of + block
            total = dot(gathered[place, 384:576, :], own[...], 1, 1)
            total += dot(gathered[place, 576:768, :], other[...], 1, 1)
            result[192 * block : 192 * block + 192, :] = total.astype(bf16)


def hidden_rows(gathered, chunk):
    half, source = chunk // 4, 2 * (chunk % 4)
    span = slice(192 * half, 192 * half + 192)
    return jnp.concatenate([gathered[source, span, :], gathered[source + 1, span, :]], axis=0)


def rows_kernel(where, features, gathered, sent, kept):
    rows_of = jnp.concatenate(
        [feature_rows(features, where[0]), feature_rows(features, where[1])], axis=0
    )
    for chunk in range(8):
        rows = hidden_rows(gathered, chunk)
        columns = slice(384 * chunk, 384 * chunk + 384)
        total = dot(rows_of, rows, 1, 1).astype(bf16)
        sent[:, columns] = total[:192]
        kept[:, columns] = total[192:]


def tokens_kernel(where, gathered, w0, w1, w2, w3, payload):
    total = None
    for chunk in range(4):
        columns = slice(768 * chunk, 768 * chunk + 768)
        rows = jnp.concatenate(
            [hidden_rows(gathered, 2 * chunk), hidden_rows(gathered, 2 * chunk + 1)], axis=0
        )
        weights = jnp.concatenate([w[:, columns] for w in (w0, w1, w2, w3)], axis=0)
        term = dot(weights, rows, 1, 0)
        total = term if total is None else total + term
    for b in range(4):
        block = total[192 * b : 192 * b + 192].astype(bf16).reshape(2, 96, 256)
        payload[pl.ds(2 * where[b], 2), 96:192, :] = block
    payload[:, 0:96, :] = jnp.zeros((8, 96, 256), bf16)


def finish_kernel(where, own, other, given, payload):
    total = own[...].astype(f32) + other[...].astype(f32)
    payload[:, 0:96, :] = total.astype(bf16).reshape(8, 96, 256)
    payload[:, 96:192, :] = given[:, 96:192, :]


def per_device(tokens, w_up, w_down, grad_out):
    xhi, core = lax.axis_index("xhi"), lax.axis_index("core")
    here = (2 * xhi + core).astype(jnp.int32)
    places = jnp.stack([here, here ^ 1, here ^ 2, here ^ 3])
    far_places = jnp.stack([here ^ 3, here ^ 2])
    near_places = jnp.stack([here ^ 1, here])
    sides = jnp.stack([xhi, core, xhi]).astype(jnp.int32)
    far_sides = jnp.stack([1 - xhi, 1 - core, xhi]).astype(jnp.int32)

    up_across = swap(w_up, "xhi")
    up_beside = swap(w_up, "core")
    up_beyond = swap(up_across, "core")
    up = (w_up, up_beside, up_across, up_beyond)
    both = jnp.concatenate([tokens.T, grad_out.T], axis=0)
    features = exchange(jnp.broadcast_to(both[None], (8, 192, 256)), "inp")
    down = natural(w_down, swap(w_down, "core"), core).reshape(1536, 768)
    g_own = features[:, 96:].reshape(768, 256)
    g_other = swap(g_own, "xhi")

    (hidden_partial,) = local(
        hidden_kernel, [(8, 384, 256)], places, features, *up, flops=4 << 30
    )
    hidden_partial, g_other = lax.optimization_barrier((hidden_partial, g_other))
    hidden = exchange(hidden_partial, wgt)
    (partial_sums,) = local(partial_kernel, [(2, 8, 192, 256)], sides, down, g_own, g_other)
    partial_sums, hidden = lax.optimization_barrier((partial_sums, hidden))
    arrived = exchange(partial_sums.reshape(16, 192, 256), ("xhi",) + wgt)
    values, slopes = local(
        gelu_kernel, [(2, 192, 256), (384, 256)], places, hidden, kinds=[bf16, f32]
    )
    crossing = swap(lax.dynamic_index_in_dim(values, 1 - xhi, 0, keepdims=False), "xhi")
    act_own = lax.dynamic_index_in_dim(values, xhi, 0, keepdims=False)
    acts = lax.optimization_barrier(jnp.concatenate([act_own, crossing], axis=0))
    grad_act = jnp.sum(arrived.reshape(2, 8, 192, 256).astype(f32), axis=1)
    grad_hidden = (grad_act * slopes.reshape(2, 192, 256)).astype(bf16).reshape(384, 256)
    portion = jnp.concatenate([grad_hidden, acts], axis=0)
    gathered = exchange(jnp.broadcast_to(portion[None], (8, 768, 256)), wgt)

    out_own, out_sent = local(output_kernel, [(768, 256)] * 2, sides, gathered, down)
    out_other = swap(out_sent, "xhi")
    gathered, out_sent = lax.optimization_barrier((gathered, out_sent))
    row_outs = [(192, 3072)] * 2
    sent, kept = local(rows_kernel, row_outs, far_places, features, gathered)
    gathered, sent, kept = lax.optimization_barrier((gathered, sent, kept))
    beyond = swap(sent, "core")
    (last,) = local(tokens_kernel, [(8, 192, 256)], places, gathered, *up, flops=4 << 30)
    near_sent, near_kept = local(
        rows_kernel, row_outs, near_places, features, gathered, flops=4 << 30
    )
    crossing = (kept.astype(f32) + beyond.astype(f32)).astype(bf16)
    last, crossing, gathered, near_sent, near_kept = lax.optimization_barrier(
        (last, crossing, gathered, near_sent, near_kept)
    )
    crossed = swap(crossing, "xhi")
    (last,) = local(finish_kernel, [(8, 192, 256)], places, out_own, out_other, last)
    last = exchange(last, "inp")
    sums = jnp.sum(last.astype(f32), axis=0).astype(bf16)
    near = near_kept.astype(f32) + swap(near_sent, "core").astype(f32)
    grad_up = (lax.optimization_barrier(near) + crossed.astype(f32)).astype(bf16)
    down_sent, down_kept = local(
        down_kernel, [(768, 768)] * 2, sides, gathered, g_own, g_other, flops=4 << 30
    )
    grad_down = (down_kept.astype(f32) + swap(down_sent, "core").astype(f32)).astype(bf16)
    return (sums[:96].T, sums[96:].T, grad_up, grad_down)


def solution(mesh):
    fine = Mesh(
        np.asarray(mesh.devices).reshape(8, 2, 4, 2, 2), ("inp", "xlo", "y", "xhi", "core")
    )
    out = ("xhi", "core")
    tok = P(out, wgt + ("inp",))
    up = P(wgt + out, "inp")
    down = P(("inp",) + out, wgt)
    return jax.shard_map(
        per_device,
        mesh=fine,
        in_specs=(tok, up, down, tok),
        out_specs=(tok, tok, up, down),
        check_vma=False,
    )
```

```python
import jax
import jax.numpy as jnp
import numpy as np
from jax import lax
from jax.experimental import pallas as pl
from jax.experimental.pallas import tpu as pltpu
from jax.sharding import Mesh, PartitionSpec as P

tanh_scale = 0.7978845608028654
cubic_weight = 0.044715
pair = [(0, 1), (1, 0)]
wgt = ("xlo", "y")
bf16, f32 = jnp.bfloat16, jnp.float32


def gelu_both(hidden):
    tangent = jnp.tanh(tanh_scale * (hidden + cubic_weight * hidden * hidden * hidden))
    value = 0.5 * hidden * (1.0 + tangent)
    slope = 0.5 * (1.0 + tangent) + 0.5 * hidden * (1.0 - tangent * tangent) * tanh_scale * (
        1.0 + 3.0 * cubic_weight * hidden * hidden
    )
    return value, slope


def dot(former, latter, former_dim, latter_dim):
    return lax.dot_general(
        former,
        latter,
        (((former_dim,), (latter_dim,)), ((), ())),
        preferred_element_type=f32,
    )


def swap(value, axis):
    return lax.ppermute(value, axis, pair)


def exchange(value, axis):
    return lax.all_to_all(value, axis, 0, 0, tiled=True)


def natural(own, other, place):
    return jnp.where(place == 0, jnp.stack([own, other]), jnp.stack([other, own]))


def local(kernel, outs, *operands, kinds=None, flops=1 << 20):
    whole = pl.BlockSpec(memory_space=pltpu.VMEM)
    kinds = kinds or [bf16] * len(outs)
    return pl.pallas_call(
        kernel,
        out_shape=[jax.ShapeDtypeStruct(shape, kind) for shape, kind in zip(outs, kinds)],
        in_specs=[pl.BlockSpec(memory_space=pltpu.SMEM)] + [whole] * (len(operands) - 1),
        out_specs=[whole] * len(outs),
        compiler_params=pltpu.CompilerParams(vmem_limit_bytes=16 * 1024 * 1024),
        cost_estimate=pl.CostEstimate(flops=flops, bytes_accessed=1 << 16, transcendentals=0),
    )(*operands)


def feature_rows(features, block):
    return features[pl.ds(2 * block, 2), 0:96, :].reshape(192, 256)


def hidden_kernel(where, features, w0, w1, w2, w3, out):
    turned = [feature_rows(features, where[b]).T for b in range(4)]
    for chunk in range(8):
        columns = slice(384 * chunk, 384 * chunk + 384)
        total = dot(turned[0], w0[:, columns], 1, 0)
        for b, weights in ((1, w1), (2, w2), (3, w3)):
            total += dot(turned[b], weights[:, columns], 1, 0)
        rows = total.astype(bf16).T
        half, target = chunk // 4, 2 * (chunk % 4)
        span = slice(192 * half, 192 * half + 192)
        out[target, span, :] = rows[:192]
        out[target + 1, span, :] = rows[192:]


def partial_kernel(where, down, own, other, partial_sums):
    for side, cotangents in ((where[0], own), (1 - where[0], other)):
        for block in range(8):
            rows = down[192 * block : 192 * block + 192, :]
            partial_sums[side, block] = dot(rows, cotangents[...], 1, 0).astype(bf16)


def gelu_kernel(where, arrived, values, slopes):
    for half in range(2):
        span = slice(192 * half, 192 * half + 192)
        hidden = arrived[0, span, :].astype(f32)
        for source in range(1, 8):
            hidden += arrived[source, span, :].astype(f32)
        value, slope = gelu_both(hidden)
        values[half] = value.astype(bf16)
        slopes[span, :] = slope


def output_kernel(where, gathered, down, own, sent):
    for result, first in ((sent, 576), (own, 384)):
        total = dot(down[0:192, :], gathered[0, first : first + 192, :], 0, 0)
        for block in range(1, 8):
            hidden = gathered[block, first : first + 192, :]
            total += dot(down[192 * block : 192 * block + 192, :], hidden, 0, 0)
        result[...] = total.astype(bf16)


def down_kernel(where, gathered, own, other, sent, kept):
    for result, rows_of in ((sent, 1 - where[1]), (kept, where[1])):
        for block in range(4):
            place = 4 * rows_of + block
            total = dot(gathered[place, 384:576, :], own[...], 1, 1)
            total += dot(gathered[place, 576:768, :], other[...], 1, 1)
            result[192 * block : 192 * block + 192, :] = total.astype(bf16)


def hidden_rows(gathered, chunk):
    half, source = chunk // 4, 2 * (chunk % 4)
    span = slice(192 * half, 192 * half + 192)
    return jnp.concatenate([gathered[source, span, :], gathered[source + 1, span, :]], axis=0)


def rows_kernel(where, features, gathered, sent, kept):
    rows_of = jnp.concatenate(
        [feature_rows(features, where[0]), feature_rows(features, where[1])], axis=0
    )
    for chunk in range(8):
        rows = hidden_rows(gathered, chunk)
        columns = slice(384 * chunk, 384 * chunk + 384)
        total = dot(rows_of, rows, 1, 1).astype(bf16)
        sent[:, columns] = total[:192]
        kept[:, columns] = total[192:]


def add_kernel(where, near, crossed, total):
    total[...] = (near[...] + crossed[...].astype(f32)).astype(bf16)


def tokens_kernel(where, gathered, w0, w1, w2, w3, payload):
    total = None
    for chunk in range(4):
        columns = slice(768 * chunk, 768 * chunk + 768)
        rows = jnp.concatenate(
            [hidden_rows(gathered, 2 * chunk), hidden_rows(gathered, 2 * chunk + 1)], axis=0
        )
        weights = jnp.concatenate([w[:, columns] for w in (w0, w1, w2, w3)], axis=0)
        term = dot(weights, rows, 1, 0)
        total = term if total is None else total + term
    for b in range(4):
        block = total[192 * b : 192 * b + 192].astype(bf16).reshape(2, 96, 256)
        payload[pl.ds(2 * where[b], 2), 96:192, :] = block
    payload[:, 0:96, :] = jnp.zeros((8, 96, 256), bf16)


def finish_kernel(where, own, other, given, payload):
    total = own[...].astype(f32) + other[...].astype(f32)
    payload[:, 0:96, :] = total.astype(bf16).reshape(8, 96, 256)
    payload[:, 96:192, :] = given[:, 96:192, :]


def per_device(tokens, w_up, w_down, grad_out):
    xhi, core = lax.axis_index("xhi"), lax.axis_index("core")
    here = (2 * xhi + core).astype(jnp.int32)
    places = jnp.stack([here, here ^ 1, here ^ 2, here ^ 3])
    far_places = jnp.stack([here ^ 3, here ^ 2])
    near_places = jnp.stack([here ^ 1, here])
    sides = jnp.stack([xhi, core, xhi]).astype(jnp.int32)
    far_sides = jnp.stack([1 - xhi, 1 - core, xhi]).astype(jnp.int32)

    up_across = swap(w_up, "xhi")
    up_beside = swap(w_up, "core")
    up_beyond = swap(up_across, "core")
    up = (w_up, up_beside, up_across, up_beyond)
    both = jnp.concatenate([tokens.T, grad_out.T], axis=0)
    features = exchange(jnp.broadcast_to(both[None], (8, 192, 256)), "inp")
    down = natural(w_down, swap(w_down, "core"), core).reshape(1536, 768)
    g_own = features[:, 96:].reshape(768, 256)
    g_other = swap(g_own, "xhi")

    (hidden_partial,) = local(
        hidden_kernel, [(8, 384, 256)], places, features, *up, flops=4 << 30
    )
    hidden_partial, g_other = lax.optimization_barrier((hidden_partial, g_other))
    hidden = exchange(hidden_partial, wgt)
    (partial_sums,) = local(partial_kernel, [(2, 8, 192, 256)], sides, down, g_own, g_other)
    partial_sums, hidden = lax.optimization_barrier((partial_sums, hidden))
    arrived = exchange(partial_sums.reshape(16, 192, 256), ("xhi",) + wgt)
    values, slopes = local(
        gelu_kernel, [(2, 192, 256), (384, 256)], places, hidden, kinds=[bf16, f32]
    )
    crossing = swap(lax.dynamic_index_in_dim(values, 1 - xhi, 0, keepdims=False), "xhi")
    act_own = lax.dynamic_index_in_dim(values, xhi, 0, keepdims=False)
    acts = lax.optimization_barrier(jnp.concatenate([act_own, crossing], axis=0))
    grad_act = jnp.sum(arrived.reshape(2, 8, 192, 256).astype(f32), axis=1)
    grad_hidden = (grad_act * slopes.reshape(2, 192, 256)).astype(bf16).reshape(384, 256)
    portion = jnp.concatenate([grad_hidden, acts], axis=0)
    gathered = exchange(jnp.broadcast_to(portion[None], (8, 768, 256)), wgt)

    out_own, out_sent = local(output_kernel, [(768, 256)] * 2, sides, gathered, down)
    out_other = swap(out_sent, "xhi")
    gathered, out_sent = lax.optimization_barrier((gathered, out_sent))
    row_outs = [(192, 3072)] * 2
    sent, kept = local(rows_kernel, row_outs, far_places, features, gathered)
    gathered, sent, kept = lax.optimization_barrier((gathered, sent, kept))
    beyond = swap(sent, "core")
    (last,) = local(tokens_kernel, [(8, 192, 256)], places, gathered, *up, flops=4 << 30)
    near_sent, near_kept = local(
        rows_kernel, row_outs, near_places, features, gathered, flops=4 << 30
    )
    crossing = (kept.astype(f32) + beyond.astype(f32)).astype(bf16)
    last, crossing, gathered, near_sent, near_kept = lax.optimization_barrier(
        (last, crossing, gathered, near_sent, near_kept)
    )
    crossed = swap(crossing, "xhi")
    (last,) = local(finish_kernel, [(8, 192, 256)], places, out_own, out_other, last)
    last = exchange(last, "inp")
    sums = jnp.sum(last.astype(f32), axis=0).astype(bf16)
    near = near_kept.astype(f32) + swap(near_sent, "core").astype(f32)
    (grad_up,) = local(add_kernel, [(192, 3072)], places, near, crossed)
    down_sent, down_kept = local(
        down_kernel, [(768, 768)] * 2, sides, gathered, g_own, g_other, flops=4 << 30
    )
    grad_down = (down_kept.astype(f32) + swap(down_sent, "core").astype(f32)).astype(bf16)
    return (sums[:96].T, sums[96:].T, grad_up, grad_down)


def solution(mesh):
    fine = Mesh(
        np.asarray(mesh.devices).reshape(8, 2, 4, 2, 2), ("inp", "xlo", "y", "xhi", "core")
    )
    out = ("xhi", "core")
    tok = P(out, wgt + ("inp",))
    up = P(wgt + out, "inp")
    down = P(("inp",) + out, wgt)
    return jax.shard_map(
        per_device,
        mesh=fine,
        in_specs=(tok, up, down, tok),
        out_specs=(tok, tok, up, down),
        check_vma=False,
    )
```
